32 devices in a mesh: parts: 2 (over y), owner: 8 (over z, core), rep: 2 (over x), sub: 1.
Axes of the slice: x: 2, y: 2, z: 4, core: 2. Of those that a mesh axis runs over, the one named last changes fastest.
Arguments:
- entity_rows: float32 [16384, 256], P(('parts', 'owner', 'rep', 'sub')), parts along dimension 0, may hold values from -1.5 to 1.5
- adagrad_sum: float32 [16384], P(('parts', 'owner', 'rep', 'sub')), parts along dimension 0, may hold values from 0.01 to 1
- src_local: int32 [16384], P(('parts', 'owner', 'rep', 'sub')), parts along dimension 0, may hold values from 0 to 511
- dst_part: int32 [16384, 1], P(('parts', 'owner', 'rep', 'sub')), parts along dimension 0, may hold values from 0 to 7; in each aligned block of 512 rows (0 to 511, 512 to 1023, ...) at most 96 rows name the same one
- dst_local: int32 [16384], P(('parts', 'owner', 'rep', 'sub')), parts along dimension 0, may hold values from 0 to 511
- rel_ids: int32 [16384], P(('parts', 'owner', 'rep', 'sub')), parts along dimension 0, may hold values from 0 to 1279
- neg_local: int32 [16384], P(('parts', 'owner', 'rep', 'sub')), parts along dimension 0, may hold values from 0 to 511
- edge_count: int32 [32], P(('parts', 'owner', 'rep', 'sub')), parts along dimension 0, may hold values from 32 to 512, as said below
- relations: float32 [1280, 256], replicated, may hold values from 0.1 to 1.9
Outputs:
- rows_new: float32 [16384, 256], P(('parts', 'owner', 'rep', 'sub')), parts along dimension 0
- adagrad_new: float32 [16384], P(('parts', 'owner', 'rep', 'sub')), parts along dimension 0
- relation_grad: float32 [2560, 256], P(('parts', 'owner', 'rep', 'sub')), parts along dimension 0
The draws below stay inside these ranges and needn't reach their ends.
There are 2 independent parts, one for each index of `parts`. The reference program is written for one: setup_inputs(seed, part) draws one part's arguments, and reference() takes and returns one part's arrays. A program takes and returns all parts, laid end to end along the dimension named above; an argument that names none is the same for every part. Nothing has to cross between parts.
Inputs may be any that keep to these rules, and one draw needn't show every extreme that they name: `dst_part`: among the edges of one task no partition is named more than 96 times; in some tasks one partition is named exactly 96 times. `edge_count`: some task has all 512 edges active and some task only 32.
All inputs are finite; a program needn't handle non-finite values.
Results may differ from the reference program's by a relative error of at most 0.0003.
Values sent between devices are 32-bit elements; how exact they have to be, the bound alone decides.
A program may use at most 64 MiB of HBM per device.

```python
import math
import jax
import jax.numpy as jnp
import numpy as np
from jax import lax

D = 256
RELS = 1280
NEG = 512
ROWS_DEV = 512
EDGES_DEV = 512
PARTITIONS = 8
INNER = 2
TASKS = 16
SLOTS = 96
ENT = 8192
EDGES = 8192
NEGS_ALL = 8192


def draw_edge_count(key, part):
    key = jax.random.fold_in(key, 7)
    first_key, second_key = jax.random.split(key)
    counts = 3 * EDGES_DEV // 4 + jax.random.randint(first_key, (TASKS,), 0, EDGES_DEV // 4 + 1)
    full_spot = jax.random.randint(second_key, (), 0, TASKS)
    counts = counts.at[full_spot].set(EDGES_DEV)
    counts = counts.at[(full_spot + 1) % TASKS].set(EDGES_DEV // 16)
    return counts.astype(jnp.int32)


def plant(drawn, stream_key, low, largest):
    longest = drawn.shape.index(max(drawn.shape))
    spots = []
    for shift in (0, 1):
        where = [jax.random.randint(jax.random.fold_in(stream_key, axis), (), 0, length) for axis, length in enumerate(drawn.shape)]
        where[longest] = (where[longest] + shift) % drawn.shape[longest]
        spots.append(tuple(where))
    return drawn.at[spots[0]].set(low).at[spots[1]].set(largest)


def levels(rng, dims, cuts, smallest, top_value):
    def one(dim, parts):
        heights = jax.random.uniform(jax.random.fold_in(jax.random.fold_in(rng, 6), dim), (parts,), jnp.float32, smallest / len(cuts), top_value / len(cuts))
        return jnp.repeat(jnp.exp(heights), dims[dim] // parts).reshape((-1,) + (1,) * (len(dims) - dim - 1))

    factor_of = one(*cuts[0])
    for cut in cuts[1:]:
        factor_of = factor_of * one(*cut)
    return factor_of


def rank_bounds(amount, skew):
    loads = [(1 << 20) // math.isqrt(standing ** skew) + 1 for standing in range(1, amount + 1)]
    spread = 1 + sum(loads) // (1 << 30)
    return np.cumsum(np.array([max(1, weight // spread) for weight in loads]))


def skewed_ids(stream_key, extent, number_of, slope):
    table = rank_bounds(number_of, slope)
    ticket = jax.random.randint(jax.random.fold_in(stream_key, 1), extent, 0, int(table[number_of - 1]))
    rank = jnp.searchsorted(jnp.asarray(table, jnp.int32), ticket, side="right")
    return jax.random.permutation(jax.random.fold_in(stream_key, 2), number_of)[rank].astype(jnp.int32)


def shared_out(rng, own, number, rows, count, top, bound, skew):
    order = jax.random.permutation(rng, count)
    crowded, usual = load_shares(count, rows * top, bound, skew, True), load_shares(count, rows * top, bound, skew, False)
    places = jnp.arange(count)

    def named(tallies, rotation):
        used = int((tallies > 0).sum())
        fixed = max(1, used // 4)
        passed = fixed + (places - fixed + rotation * (used - fixed)) % max(1, count - fixed)
        return jnp.zeros((count,), jnp.int32).at[order[jnp.where(places < fixed, places, passed)]].set(jnp.asarray(tallies, jnp.int32))

    tallies = jnp.where(number % 4 == 0, named(crowded, number // 4), named(usual, number - number // 4 - 1))
    mixed = jax.random.permutation(jax.random.fold_in(own, 3), count)
    giver, receiver = mixed[0:count // 2 * 2:2], mixed[1:count // 2 * 2:2]
    slack = jnp.minimum(tallies[giver] - 1, bound - tallies[receiver]) // 2
    slack = jnp.where((giver == order[0]) | (receiver == order[0]) | (tallies[receiver] == 0), 0, jnp.maximum(slack, 0))
    passed = jax.random.randint(jax.random.fold_in(own, 4), (count // 2,), 0, 1 << 20) % (slack + 1)
    tallies = tallies.at[giver].add(-passed).at[receiver].add(passed)
    labels = jnp.searchsorted(jnp.cumsum(tallies), jnp.arange(rows * top), side="right").astype(jnp.int32)
    grid = labels.reshape(top, rows).T
    grid = grid[jax.random.permutation(jax.random.fold_in(own, 1), rows)]
    rotation = jax.random.randint(jax.random.fold_in(own, 2), (rows, 1), 0, top)
    return jnp.take_along_axis(grid, (jnp.arange(top)[None, :] + rotation) % top, axis=1)


def load_shares(count, total, reach, slope, full):
    loads = [(1 << 20) // math.isqrt(rank ** slope) + 1 for rank in range(1, count + 1)]
    largest = reach if full else min(reach, max(-(-total // count), total * loads[0] // sum(loads)))
    least = 1 if total - largest >= count - 1 else 0
    holding, surplus = [largest] + [least] * (count - 1), total - largest - least * (count - 1)
    while surplus > 0:
        movable = [i for i in range(1, count) if holding[i] < largest] or [i for i in range(1, count) if holding[i] < reach]
        whole, budget = sum([loads[i] for i in movable]), surplus
        for i in movable:
            extra = min(reach - holding[i], max(1, budget * loads[i] // whole), surplus)
            holding[i] = holding[i] + extra
            surplus = surplus - extra
    return np.array(holding)


def bell_draw(key, shape, spread, most, cuts=(), kind=jnp.bfloat16):
    values = spread * jax.random.normal(key, shape, jnp.float32)
    if cuts:
        values = values * levels(key, shape, cuts, -0.22, 0.18)
    return jnp.clip(values, -most, most).astype(kind)


def setup_inputs(seed: int = 0, part: int = 0) -> dict:
    arg_keys = jax.random.split(jax.random.key(seed), 10)
    part_keys = jax.random.split(jax.random.fold_in(arg_keys[9], part), 10)
    entity_rows = bell_draw(part_keys[0], (ENT, D), 0.25, 1.5, ((0, 16),), jnp.float32)
    adagrad_sum = jnp.clip(jnp.exp(math.log(1.0) - 4.6051702 * jax.random.uniform(part_keys[1], (ENT,), jnp.float32) ** levels(part_keys[1], (ENT,), ((0, 16),), -0.2, 0.2)), 0.01, 1.0)
    src_local = plant(jax.random.randint(part_keys[2], (EDGES,), 0, ROWS_DEV), jax.random.fold_in(part_keys[2], 1), 0, ROWS_DEV - 1).astype(jnp.int32)
    dst_part_keys = jax.random.split(jax.random.fold_in(part_keys[3], 1), EDGES // EDGES_DEV)
    dst_part_turns = jax.random.permutation(jax.random.fold_in(part_keys[3], 3), EDGES // EDGES_DEV)
    dst_part = jax.vmap(lambda own, number: shared_out(jax.random.fold_in(part_keys[3], 2), own, number, EDGES_DEV, PARTITIONS, 1, SLOTS, 2))(dst_part_keys, dst_part_turns).reshape((EDGES, 1))
    dst_local = plant(jax.random.randint(part_keys[4], (EDGES,), 0, ROWS_DEV), jax.random.fold_in(part_keys[4], 1), 0, ROWS_DEV - 1).astype(jnp.int32)
    rel_ids = plant(skewed_ids(part_keys[5], (EDGES,), RELS, 2), jax.random.fold_in(part_keys[5], 3), 0, RELS - 1).astype(jnp.int32)
    neg_local = plant(jax.random.randint(part_keys[6], (NEGS_ALL,), 0, ROWS_DEV), jax.random.fold_in(part_keys[6], 1), 0, ROWS_DEV - 1).astype(jnp.int32)
    edge_count = draw_edge_count(jax.random.fold_in(jax.random.fold_in(arg_keys[9], part), 71), part)
    relations = jnp.clip(1.0 + 0.18 * jax.random.normal(arg_keys[8], (RELS, D), jnp.float32), 0.1, 1.9)
    return {"entity_rows": entity_rows, "adagrad_sum": adagrad_sum, "src_local": src_local, "dst_part": dst_part, "dst_local": dst_local, "rel_ids": rel_ids, "neg_local": neg_local, "edge_count": edge_count, "relations": relations}


step_size = 0.1

def reference(entity_rows, adagrad_sum, src_local, dst_part, dst_local, rel_ids, neg_local, edge_count, relations):
    task_ids = jnp.arange(TASKS, dtype=jnp.int32)
    src_all = src_local.reshape(TASKS, EDGES_DEV)
    part_all = dst_part.reshape(TASKS, EDGES_DEV)
    dloc_all = dst_local.reshape(TASKS, EDGES_DEV)
    rel_all = rel_ids.reshape(TASKS, EDGES_DEV)
    neg_all = neg_local.reshape(TASKS, NEG)

    def task_step(totals, inputs):
        grad_rows, grad_rel = totals
        task_id, src_t, part_t, dloc_t, rel_t, neg_t, live_count = inputs
        row_base = task_id * ROWS_DEV
        src_idx = (row_base + src_t).astype(jnp.int32)
        dst_idx = ((part_t * INNER + task_id % INNER) * ROWS_DEV + dloc_t).astype(jnp.int32)
        neg_idx = (row_base + neg_t).astype(jnp.int32)
        source = entity_rows[src_idx]
        target = entity_rows[dst_idx]
        negatives = entity_rows[neg_idx]
        operator = relations[rel_t]
        queries = source * operator
        neg_scores = jnp.dot(queries, negatives.T, precision=lax.Precision.HIGHEST, preferred_element_type=jnp.float32)
        positive = lax.optimization_barrier(jnp.sum(queries * target, axis=1))
        active = (jnp.arange(EDGES_DEV, dtype=jnp.int32) < live_count).astype(entity_rows.dtype)
        grad_pos = -jax.nn.sigmoid(-positive) * active
        grad_neg = jax.nn.sigmoid(neg_scores) * (active / NEG)[:, None]
        grad_target = grad_pos[:, None] * queries
        grad_query = grad_pos[:, None] * target + jnp.dot(grad_neg, negatives, precision=lax.Precision.HIGHEST, preferred_element_type=jnp.float32)
        grad_source = grad_query * operator
        grad_operator = grad_query * source
        grad_negative = jnp.dot(grad_neg.T, queries, precision=lax.Precision.HIGHEST, preferred_element_type=jnp.float32)
        grad_rows = grad_rows.at[src_idx].add(grad_source).at[dst_idx].add(grad_target).at[neg_idx].add(grad_negative)
        grad_rel = grad_rel.at[rel_t].add(grad_operator)
        return ((grad_rows, grad_rel), None)
    start = (jnp.zeros(entity_rows.shape, entity_rows.dtype), jnp.zeros(relations.shape, relations.dtype))
    (grad_rows, relation_grad), _ = lax.scan(task_step, start, (task_ids, src_all, part_all, dloc_all, rel_all, neg_all, edge_count))
    adagrad_new = adagrad_sum + lax.optimization_barrier(jnp.mean(grad_rows * grad_rows, axis=1))
    rows_new = entity_rows - step_size * grad_rows / jnp.sqrt(adagrad_new)[:, None]
    return (rows_new, adagrad_new, relation_grad)
```

```python
import functools

import jax
import jax.numpy as jnp
from jax import lax
from jax.experimental import pallas as pl
from jax.experimental.pallas import tpu as pltpu
from jax.sharding import PartitionSpec as P

step_size = 0.1
F32 = jnp.float32
BF16 = jnp.bfloat16
MESH = pl.DeviceIdType.MESH


def iota(shape, dim):
    return lax.broadcasted_iota(jnp.int32, shape, dim).astype(F32)


def dot(a, b):
    return lax.dot_general(a, b, (((1,), (0,)), ((), ())), preferred_element_type=F32)


def dot_nt(a, b):
    return lax.dot_general(a, b, (((1,), (1,)), ((), ())), preferred_element_type=F32)


def split(x):
    hi = x.astype(BF16)
    return hi, (x - hi.astype(F32)).astype(BF16)


def put_split(ref, rows, x):
    width = x.shape[1]
    hi, lo = split(x)
    ref[rows, 0:width] = hi
    ref[rows, width:] = lo


def fold(x):
    width = x.shape[1] // 2
    return x[:, :width] + x[:, width:]


def onehot(a, b):
    return jnp.where(a == b, 1.0, 0.0).astype(BF16)


def each(count, step):
    if count <= 8:
        for k in range(count):
            step(k)
    else:

        @pl.loop(0, count)
        def _(k):
            step(k)


def kernel(
    dims,
    ent,
    ada,
    src,
    dpart,
    dloc,
    rel,
    neg,
    cnt,
    relations,
    rows_out,
    ada_out,
    rel_out,
    ids_out,
    ids_in,
    ent_hl,
    rel_hl,
    neg_hl,
    served,
    fetched,
    outgoing,
    incoming,
    q_s,
    source_s,
    oper_s,
    gq_s,
    q_hl,
    go_hl,
    act_s,
    frow,
    gneg,
    rel_part,
    recv1,
    recv2,
    recv3,
    ids_send,
    ids_recv,
    row_send,
    row_recv,
    grad_send,
    grad_recv,
    s1_send,
    s1_recv,
    s2_send,
    s2_recv,
    s3_send,
    s3_recv,
):
    n, reps, subs, cores, zs, cap, shard, pad = dims
    me = lax.axis_index("owner")
    x = lax.axis_index("rep")
    edges = src.shape[1]
    rows, width = ent.shape
    slots = n * cap
    rels = relations.shape[0]
    chunk = 256 if slots % 256 == 0 else slots
    if subs > 1:
        c, z = lax.axis_index("sub"), me
    else:
        c, z = lax.rem(me, cores), lax.div(me, cores)

    def owner_peer(k):
        return lax.rem(me + k, n)

    def core_peer(k):
        p = lax.rem(c + k, cores)
        return p, ({"sub": p} if subs > 1 else {"owner": z * cores + p})

    def rep_peer(k):
        p = lax.rem(x + k, reps)
        return p, {"rep": p}

    def z_peer(k):
        p = lax.rem(z + k, zs)
        return p, ({"owner": p} if subs > 1 else {"owner": p * cores + c})

    barrier = pltpu.get_barrier_semaphore()

    def greet(device):
        pl.semaphore_signal(barrier, inc=1, device_id=device, device_id_type=MESH)

    each(n - 1, lambda k: greet({"owner": owner_peer(k + 1)}))
    each(reps - 1, lambda k: greet(rep_peer(k + 1)[1]))
    greeted = n - 1 + reps - 1
    if subs > 1:
        each(subs - 1, lambda k: greet(core_peer(k + 1)[1]))
        greeted += subs - 1

    def copy(source, target, send, recv, device):
        return pltpu.make_async_remote_copy(
            src_ref=source,
            dst_ref=target,
            send_sem=send,
            recv_sem=recv,
            device_id=device,
            device_id_type=MESH,
        )

    def ids_copy(p, s):
        return copy(ids_out.at[p], ids_in.at[s], ids_send.at[p], ids_recv.at[s], {"owner": p})

    def row_copy(p, s):
        return copy(served.at[p], fetched.at[s], row_send.at[p], row_recv.at[s], {"owner": p})

    def grad_copy(p, s):
        return copy(outgoing.at[p], incoming.at[s], grad_send.at[p], grad_recv.at[s], {"owner": p})

    dpart_row = dpart[...].astype(F32)
    pt = iota((n, edges), 0) == dpart_row
    before = dot(
        jnp.where(pt, 1.0, 0.0).astype(BF16),
        jnp.where(iota((edges, edges), 0) < iota((edges, edges), 1), 1.0, 0.0).astype(BF16),
    )
    rank = jnp.sum(jnp.where(pt, before, 0.0), axis=0, keepdims=True)
    slot_row = dpart_row * cap + rank

    def low_high(ref):
        v = ref[...]
        return (v & 255).astype(F32), (v >> 8).astype(F32)

    rt = onehot(iota((128, edges), 0), rank)
    low, high = low_high(dloc)
    wanted = dot_nt(jnp.where(pt, low, 0.0).astype(BF16), rt) + 256.0 * dot_nt(
        jnp.where(pt, high, 0.0).astype(BF16), rt
    )
    for p in range(n):
        ids_out[p] = wanted[p : p + 1, :]
    pl.semaphore_wait(barrier, greeted)
    each(n - 1, lambda k: ids_copy(owner_peer(k + 1), me).start())
    ids_in[me] = ids_out[me]

    put_split(ent_hl, pl.ds(0, rows), ent[...])

    def id_column(s):
        return jnp.transpose(jnp.broadcast_to(ids_in[s], (8, 128)))[:cap, 0:1]

    def serve(s):
        return fold(dot(onehot(id_column(s), iota((cap, rows), 1)), ent_hl[...]))

    def serve_peer(k):
        p = owner_peer(k + 1)
        ids_copy(p, p).wait_recv()
        served[p] = serve(p)
        row_copy(p, me).start()

    each(n - 1, serve_peer)
    fetched[me] = serve(me)

    src_low, src_high = low_high(src)
    rel_low, rel_high = low_high(rel)
    active = jnp.where(
        lax.broadcasted_iota(jnp.int32, (1, edges), 1) < cnt[...], 1.0, 0.0
    )
    fields = jnp.concatenate(
        [src_low, src_high, rel_low, rel_high, active, jnp.zeros((11, edges), F32)], axis=0
    ).astype(BF16)
    for t in range(rels // 256):
        put_split(rel_hl, pl.ds(t * 256, 256), relations[pl.ds(t * 256, 256), :])
    neg_col = jnp.transpose(jnp.broadcast_to(neg[...].astype(F32), (8, edges)))[:, 0:1]
    neg_hl[...] = dot(onehot(neg_col, iota((edges, rows), 1)), ent_hl[...]).astype(BF16)
    gneg[...] = jnp.zeros_like(gneg)

    @pl.loop(0, slots // chunk)
    def _(t):
        at = pl.ds(pl.multiple_of(t * chunk, chunk), chunk)
        first = (t * chunk).astype(F32)
        st = onehot(iota((chunk, edges), 0) + first, slot_row)
        fcol = dot_nt(st, fields)
        frow[:, at] = dot_nt(fields, st)
        src_col = fcol[:, 0:1] + 256.0 * fcol[:, 1:2]
        rel_col = fcol[:, 2:3] + 256.0 * fcol[:, 3:4]
        act_col = fcol[:, 4:5]
        act_s[at, :] = act_col
        source = fold(dot(onehot(src_col, iota((chunk, rows), 1)), ent_hl[...]))
        operator = fold(dot(onehot(rel_col, iota((chunk, rels), 1)), rel_hl[...]))
        queries = source * operator
        source_s[at, :] = source
        oper_s[at, :] = operator
        q_s[at, :] = queries
        q_hi, q_lo = split(queries)
        q_hl[:, :width] = q_hi
        q_hl[:, width:] = q_lo
        n_hi = neg_hl[:, :width]
        n_lo = neg_hl[:, width:]
        scores = dot_nt(q_hi, n_hi) + (dot_nt(q_hi, n_lo) + dot_nt(q_lo, n_hi))
        gn = jax.nn.sigmoid(scores) * (act_col / edges_neg(neg))
        gn_hi, gn_lo = split(gn)
        gq_s[at, :] = fold(dot(gn_hi, neg_hl[...])) + dot(gn_lo, n_hi)
        gt_hi, gt_lo = split(jnp.transpose(gn))
        gneg[...] += fold(dot(gt_hi, q_hl[...])) + dot(gt_lo, q_hi)

    def block_rows(p):
        return pl.ds(pl.multiple_of(p * cap, 8), cap)

    def score(p, out):
        at = block_rows(p)
        target = fetched[p]
        queries = q_s[at, :]
        positive = jnp.sum(queries * target, axis=1, keepdims=True)
        grad_pos = -jax.nn.sigmoid(-positive) * act_s[at, :]
        out[...] = grad_pos * queries
        gq_s[at, :] += grad_pos * target

    score(me, incoming.at[me])

    def score_peer(k):
        p = owner_peer(n - 1 - k)
        row_copy(p, p).wait_recv()
        score(p, outgoing.at[p])
        grad_copy(p, me).start()

    each(n - 1, score_peer)

    for t in range(slots // chunk):
        at = pl.ds(t * chunk, chunk)
        put_split(go_hl, at, gq_s[at, :] * source_s[at, :])
    rel_row = frow[2:3, :] + 256.0 * frow[3:4, :]
    block = zs * pad

    def rel_block(cc, xx):
        local = iota((block, 1), 0)
        zz = jnp.floor((local + 0.5) * (1.0 / pad))
        within = local - zz * pad
        cf, xf = cc.astype(F32), xx.astype(F32)
        if subs > 1:
            dev = (zz * reps + xf) * subs + cf
        else:
            dev = (zz * cores + cf) * reps + xf
        ident = jnp.where(within < shard, dev * shard + within, -1.0)
        rel_part[cc, xx] = fold(dot(onehot(ident, rel_row), go_hl[...]))

    def s1_copy(p, device, s):
        return copy(rel_part.at[p], recv1.at[s], s1_send.at[p], s1_recv.at[s], device)

    def s2_copy(p, device, s):
        return copy(rel_part.at[c, p], recv2.at[s], s2_send.at[p], s2_recv.at[s], device)

    def s3_copy(p, device, s):
        return copy(
            rel_part.at[c, x, pl.ds(pl.multiple_of(p * pad, 8), pad)],
            recv3.at[s],
            s3_send.at[p],
            s3_recv.at[s],
            device,
        )

    def s1_start(k):
        p, device = core_peer(k + 1)
        for r in range(reps):
            rel_block(p, rep_peer(r)[0])
        s1_copy(p, device, c).start()

    each(cores - 1, s1_start)
    for r in range(reps):
        rel_block(c, rep_peer(r)[0])

    def s1_wait(k):
        p, device = core_peer(k + 1)
        s1_copy(p, device, p).wait_recv()
        for r in range(reps):
            rel_part[c, r] += recv1[p, r]

    each(cores - 1, s1_wait)

    def s2_start(k):
        p, device = rep_peer(k + 1)
        s2_copy(p, device, x).start()

    each(reps - 1, s2_start)

    src_row = frow[0:1, :] + 256.0 * frow[1:2, :]
    for t in range(slots // chunk):
        at = pl.ds(t * chunk, chunk)
        put_split(go_hl, at, gq_s[at, :] * oper_s[at, :])
    grad = fold(dot(onehot(iota((rows, slots), 0), src_row), go_hl[...]))
    gneg_hi, gneg_lo = split(gneg[...])
    neg_to = onehot(iota((rows, edges), 0), neg[...].astype(F32))
    gneg[...] = grad + (dot(neg_to, gneg_hi) + dot(neg_to, gneg_lo))

    def s2_wait(k):
        p, device = rep_peer(k + 1)
        s2_copy(p, device, p).wait_recv()
        rel_part[c, x] += recv2[p]

    each(reps - 1, s2_wait)

    def s3_start(k):
        p, device = z_peer(k + 1)
        s3_copy(p, device, z).start()

    each(zs - 1, s3_start)

    def gather_in(p):
        to = onehot(iota((rows, cap), 0), ids_in[p][:, :cap])
        hi, lo = split(incoming[p])
        gneg[...] += dot(to, hi) + dot(to, lo)

    gather_in(me)

    def gather_peer(k):
        p = owner_peer(k + 1)
        grad_copy(p, p).wait_recv()
        gather_in(p)

    each(n - 1, gather_peer)

    total = gneg[...]
    ada_col = jnp.transpose(jnp.broadcast_to(ada[...], (8, rows)))[:, 0:1]
    ada_new = ada_col + jnp.sum(total * total, axis=1, keepdims=True) * (1.0 / width)
    rows_out[...] = ent[...] - step_size * total / jnp.sqrt(ada_new)
    ada_out[...] = jnp.transpose(jnp.broadcast_to(ada_new, (rows, 128)))[0:1, :]

    rel_out[...] = rel_part[c, x, pl.ds(pl.multiple_of(z * pad, 8), pad)][:shard]

    def s3_wait(k):
        p, device = z_peer(k + 1)
        s3_copy(p, device, p).wait_recv()
        rel_out[...] += recv3[p][:shard]

    each(zs - 1, s3_wait)

    def drain(k):
        p = owner_peer(k + 1)
        ids_copy(p, me).wait_send()
        row_copy(p, me).wait_send()
        grad_copy(p, me).wait_send()

    each(n - 1, drain)

    def drain1(k):
        p, device = core_peer(k + 1)
        s1_copy(p, device, c).wait_send()

    def drain2(k):
        p, device = rep_peer(k + 1)
        s2_copy(p, device, x).wait_send()

    def drain3(k):
        p, device = z_peer(k + 1)
        s3_copy(p, device, z).wait_send()

    each(cores - 1, drain1)
    each(reps - 1, drain2)
    each(zs - 1, drain3)


def edges_neg(neg):
    return float(neg.shape[1])


def body(
    entity_rows,
    adagrad_sum,
    src_local,
    dst_part,
    dst_local,
    rel_ids,
    neg_local,
    edge_count,
    relations,
):
    n = lax.axis_size("owner")
    reps = lax.axis_size("rep")
    subs = lax.axis_size("sub")
    edges = src_local.shape[0]
    rows, width = entity_rows.shape
    rels = relations.shape[0]
    cap = edges // n * 3 // 2
    shard = rels // (n * reps * subs)
    pad = -(-shard // 8) * 8
    cores = subs if subs > 1 else (2 if n % 2 == 0 else 1)
    zs = n if subs > 1 else n // cores
    dims = (n, reps, subs, cores, zs, cap, shard, pad)
    slots = n * cap
    chunk = 256 if slots % 256 == 0 else slots
    vmem = pl.BlockSpec(memory_space=pltpu.VMEM)
    dma = pltpu.SemaphoreType.DMA

    def row(a):
        return a.reshape(1, -1)

    rows_new, ada_new, rel_grad = pl.pallas_call(
        functools.partial(kernel, dims),
        out_shape=(
            jax.ShapeDtypeStruct((rows, width), F32),
            jax.ShapeDtypeStruct((1, rows), F32),
            jax.ShapeDtypeStruct((shard, width), F32),
        ),
        in_specs=[vmem] * 9,
        out_specs=(vmem, vmem, vmem),
        scratch_shapes=[
            pltpu.VMEM((n, 1, 128), F32),
            pltpu.VMEM((n, 1, 128), F32),
            pltpu.VMEM((rows, 2 * width), BF16),
            pltpu.VMEM((rels, 2 * width), BF16),
            pltpu.VMEM((edges, 2 * width), BF16),
            pltpu.VMEM((n, cap, width), F32),
            pltpu.VMEM((n, cap, width), F32),
            pltpu.VMEM((n, cap, width), F32),
            pltpu.VMEM((n, cap, width), F32),
            pltpu.VMEM((slots, width), F32),
            pltpu.VMEM((slots, width), F32),
            pltpu.VMEM((slots, width), F32),
            pltpu.VMEM((slots, width), F32),
            pltpu.VMEM((chunk, 2 * width), BF16),
            pltpu.VMEM((slots, 2 * width), BF16),
            pltpu.VMEM((slots, 1), F32),
            pltpu.VMEM((16, slots), F32),
            pltpu.VMEM((rows, width), F32),
            pltpu.VMEM((cores, reps, zs * pad, width), F32),
            pltpu.VMEM((cores, reps, zs * pad, width), F32),
            pltpu.VMEM((reps, zs * pad, width), F32),
            pltpu.VMEM((zs, pad, width), F32),
            dma((n,)),
            dma((n,)),
            dma((n,)),
            dma((n,)),
            dma((n,)),
            dma((n,)),
            dma((cores,)),
            dma((cores,)),
            dma((reps,)),
            dma((reps,)),
            dma((zs,)),
            dma((zs,)),
        ],
        compiler_params=pltpu.CompilerParams(
            collective_id=0, has_side_effects=True, vmem_limit_bytes=48 * 1024 * 1024
        ),
        cost_estimate=pl.CostEstimate(
            flops=10_000_000_000, bytes_accessed=3_000_000, transcendentals=400_000
        ),
    )(
        entity_rows,
        row(adagrad_sum),
        row(src_local),
        row(dst_part),
        row(dst_local),
        row(rel_ids),
        row(neg_local),
        row(edge_count),
        relations,
    )
    return rows_new, ada_new.reshape(-1), rel_grad


def solution(mesh):
    split_rows = P(("parts", "owner", "rep", "sub"))
    split_wide = P(("parts", "owner", "rep", "sub"), None)
    in_specs = (
        split_wide,
        split_rows,
        split_rows,
        split_wide,
        split_rows,
        split_rows,
        split_rows,
        split_rows,
        P(),
    )
    out_specs = (split_wide, split_rows, split_wide)
    return jax.shard_map(body, mesh=mesh, in_specs=in_specs, out_specs=out_specs, check_vma=False)
```

```python
import functools

import jax
import jax.numpy as jnp
from jax import lax
from jax.experimental import pallas as pl
from jax.experimental.pallas import tpu as pltpu
from jax.sharding import PartitionSpec as P

step_size = 0.1
F32 = jnp.float32
BF16 = jnp.bfloat16
MESH = pl.DeviceIdType.MESH


def iota(shape, dim):
    return lax.broadcasted_iota(jnp.int32, shape, dim).astype(F32)


def dot(a, b):
    return lax.dot_general(a, b, (((1,), (0,)), ((), ())), preferred_element_type=F32)


def dot_nt(a, b):
    return lax.dot_general(a, b, (((1,), (1,)), ((), ())), preferred_element_type=F32)


def split(x):
    hi = x.astype(BF16)
    return hi, (x - hi.astype(F32)).astype(BF16)


def put_split(ref, rows, x):
    width = x.shape[1]
    hi, lo = split(x)
    ref[rows, 0:width] = hi
    ref[rows, width:] = lo


def fold(x):
    width = x.shape[1] // 2
    return x[:, :width] + x[:, width:]


def onehot(a, b):
    return jnp.where(a == b, 1.0, 0.0).astype(BF16)


def each(count, step):
    if count <= 8:
        for k in range(count):
            step(k)
    else:

        @pl.loop(0, count)
        def _(k):
            step(k)


def kernel(
    dims,
    ent_in,
    ada_in,
    src_in,
    dpart_in,
    dloc_in,
    rel_in,
    neg_in,
    cnt,
    relations_in,
    rows_out,
    ada_out,
    rel_out,
    ids_out,
    ids_in,
    ent_hl,
    rel_hl,
    neg_hl,
    served,
    fetched,
    outgoing,
    incoming,
    q_s,
    source_s,
    oper_s,
    gq_s,
    q_hl,
    go_hl,
    act_s,
    frow,
    gneg,
    rel_part,
    recv1,
    recv2,
    recv3,
    ids_send,
    ids_recv,
    row_send,
    row_recv,
    grad_send,
    grad_recv,
    s1_send,
    s1_recv,
    s2_send,
    s2_recv,
    s3_send,
    s3_recv,
    ent,
    ada,
    src,
    dpart,
    dloc,
    rel,
    neg,
    relations,
    load_sem,
):
    n, reps, subs, cores, zs, cap, shard, pad = dims
    pairs = (
        (dpart_in, dpart),
        (dloc_in, dloc),
        (ent_in, ent),
        (src_in, src),
        (rel_in, rel),
        (neg_in, neg),
        (relations_in, relations),
        (ada_in, ada),
    )
    loads = [
        pltpu.make_async_copy(a, b, load_sem.at[i]) for i, (a, b) in enumerate(pairs)
    ]
    for load in loads:
        load.start()
    me = lax.axis_index("owner")
    x = lax.axis_index("rep")
    edges = src.shape[1]
    rows, width = ent.shape
    slots = n * cap
    rels = relations.shape[0]
    chunk = 256 if slots % 256 == 0 else slots
    if subs > 1:
        c, z = lax.axis_index("sub"), me
    else:
        c, z = lax.rem(me, cores), lax.div(me, cores)

    def owner_peer(k):
        return lax.rem(me + k, n)

    def core_peer(k):
        p = lax.rem(c + k, cores)
        return p, ({"sub": p} if subs > 1 else {"owner": z * cores + p})

    def rep_peer(k):
        p = lax.rem(x + k, reps)
        return p, {"rep": p}

    def z_peer(k):
        p = lax.rem(z + k, zs)
        return p, ({"owner": p} if subs > 1 else {"owner": p * cores + c})

    barrier = pltpu.get_barrier_semaphore()

    def greet(device):
        pl.semaphore_signal(barrier, inc=1, device_id=device, device_id_type=MESH)

    each(n - 1, lambda k: greet({"owner": owner_peer(k + 1)}))
    each(reps - 1, lambda k: greet(rep_peer(k + 1)[1]))
    greeted = n - 1 + reps - 1
    if subs > 1:
        each(subs - 1, lambda k: greet(core_peer(k + 1)[1]))
        greeted += subs - 1

    def copy(source, target, send, recv, device):
        return pltpu.make_async_remote_copy(
            src_ref=source,
            dst_ref=target,
            send_sem=send,
            recv_sem=recv,
            device_id=device,
            device_id_type=MESH,
        )

    def ids_copy(p, s):
        return copy(ids_out.at[p], ids_in.at[s], ids_send.at[p], ids_recv.at[s], {"owner": p})

    def row_copy(p, s):
        return copy(served.at[p], fetched.at[s], row_send.at[p], row_recv.at[s], {"owner": p})

    def grad_copy(p, s):
        return copy(outgoing.at[p], incoming.at[s], grad_send.at[p], grad_recv.at[s], {"owner": p})

    loads[0].wait()
    loads[1].wait()
    dpart_row = dpart[...].astype(F32)
    pt = iota((n, edges), 0) == dpart_row
    before = dot(
        jnp.where(pt, 1.0, 0.0).astype(BF16),
        jnp.where(iota((edges, edges), 0) < iota((edges, edges), 1), 1.0, 0.0).astype(BF16),
    )
    rank = jnp.sum(jnp.where(pt, before, 0.0), axis=0, keepdims=True)
    slot_row = dpart_row * cap + rank

    def low_high(ref):
        v = ref[...]
        return (v & 255).astype(F32), (v >> 8).astype(F32)

    rt = onehot(iota((128, edges), 0), rank)
    low, high = low_high(dloc)
    wanted = dot_nt(jnp.where(pt, low, 0.0).astype(BF16), rt) + 256.0 * dot_nt(
        jnp.where(pt, high, 0.0).astype(BF16), rt
    )
    for p in range(n):
        ids_out[p] = wanted[p : p + 1, :]
    pl.semaphore_wait(barrier, greeted)
    each(n - 1, lambda k: ids_copy(owner_peer(k + 1), me).start())
    ids_in[me] = ids_out[me]

    loads[2].wait()
    put_split(ent_hl, pl.ds(0, rows), ent[...])

    def id_column(s):
        return jnp.transpose(jnp.broadcast_to(ids_in[s], (8, 128)))[:cap, 0:1]

    def serve(s):
        return fold(dot(onehot(id_column(s), iota((cap, rows), 1)), ent_hl[...]))

    def serve_peer(k):
        p = owner_peer(k + 1)
        ids_copy(p, p).wait_recv()
        served[p] = serve(p)
        row_copy(p, me).start()

    each(n - 1, serve_peer)
    fetched[me] = serve(me)

    for load in loads[3:]:
        load.wait()
    src_low, src_high = low_high(src)
    rel_low, rel_high = low_high(rel)
    active = jnp.where(
        lax.broadcasted_iota(jnp.int32, (1, edges), 1) < cnt[...], 1.0, 0.0
    )
    fields = jnp.concatenate(
        [src_low, src_high, rel_low, rel_high, active, jnp.zeros((11, edges), F32)], axis=0
    ).astype(BF16)
    for t in range(rels // 256):
        put_split(rel_hl, pl.ds(t * 256, 256), relations[pl.ds(t * 256, 256), :])
    neg_col = jnp.transpose(jnp.broadcast_to(neg[...].astype(F32), (8, edges)))[:, 0:1]
    neg_hl[...] = dot(onehot(neg_col, iota((edges, rows), 1)), ent_hl[...]).astype(BF16)
    gneg[...] = jnp.zeros_like(gneg)

    @pl.loop(0, slots // chunk)
    def _(t):
        at = pl.ds(pl.multiple_of(t * chunk, chunk), chunk)
        first = (t * chunk).astype(F32)
        st = onehot(iota((chunk, edges), 0) + first, slot_row)
        fcol = dot_nt(st, fields)
        frow[:, at] = dot_nt(fields, st)
        src_col = fcol[:, 0:1] + 256.0 * fcol[:, 1:2]
        rel_col = fcol[:, 2:3] + 256.0 * fcol[:, 3:4]
        act_col = fcol[:, 4:5]
        act_s[at, :] = act_col
        source = fold(dot(onehot(src_col, iota((chunk, rows), 1)), ent_hl[...]))
        operator = fold(dot(onehot(rel_col, iota((chunk, rels), 1)), rel_hl[...]))
        queries = source * operator
        source_s[at, :] = source
        oper_s[at, :] = operator
        q_s[at, :] = queries
        q_hi, q_lo = split(queries)
        q_hl[:, :width] = q_hi
        q_hl[:, width:] = q_lo
        n_hi = neg_hl[:, :width]
        n_lo = neg_hl[:, width:]
        scores = dot_nt(q_hi, n_hi) + (dot_nt(q_hi, n_lo) + dot_nt(q_lo, n_hi))
        gn = jax.nn.sigmoid(scores) * (act_col / edges_neg(neg))
        gn_hi, gn_lo = split(gn)
        gq_s[at, :] = fold(dot(gn_hi, neg_hl[...])) + dot(gn_lo, n_hi)
        gt_hi, gt_lo = split(jnp.transpose(gn))
        gneg[...] += fold(dot(gt_hi, q_hl[...])) + dot(gt_lo, q_hi)

    def block_rows(p):
        return pl.ds(pl.multiple_of(p * cap, 8), cap)

    def score(p, out):
        at = block_rows(p)
        target = fetched[p]
        queries = q_s[at, :]
        positive = jnp.sum(queries * target, axis=1, keepdims=True)
        grad_pos = -jax.nn.sigmoid(-positive) * act_s[at, :]
        out[...] = grad_pos * queries
        gq_s[at, :] += grad_pos * target

    score(me, incoming.at[me])

    def score_peer(k):
        p = owner_peer(n - 1 - k)
        row_copy(p, p).wait_recv()
        score(p, outgoing.at[p])
        grad_copy(p, me).start()

    each(n - 1, score_peer)

    for t in range(slots // chunk):
        at = pl.ds(t * chunk, chunk)
        put_split(go_hl, at, gq_s[at, :] * source_s[at, :])
    rel_row = frow[2:3, :] + 256.0 * frow[3:4, :]
    block = zs * pad

    def rel_block(cc, xx):
        local = iota((block, 1), 0)
        zz = jnp.floor((local + 0.5) * (1.0 / pad))
        within = local - zz * pad
        cf, xf = cc.astype(F32), xx.astype(F32)
        if subs > 1:
            dev = (zz * reps + xf) * subs + cf
        else:
            dev = (zz * cores + cf) * reps + xf
        ident = jnp.where(within < shard, dev * shard + within, -1.0)
        rel_part[cc, xx] = fold(dot(onehot(ident, rel_row), go_hl[...]))

    def s1_copy(p, device, s):
        return copy(rel_part.at[p], recv1.at[s], s1_send.at[p], s1_recv.at[s], device)

    def s2_copy(p, device, s):
        return copy(rel_part.at[c, p], recv2.at[s], s2_send.at[p], s2_recv.at[s], device)

    def s3_copy(p, device, s):
        return copy(
            rel_part.at[c, x, pl.ds(pl.multiple_of(p * pad, 8), pad)],
            recv3.at[s],
            s3_send.at[p],
            s3_recv.at[s],
            device,
        )

    def s1_start(k):
        p, device = core_peer(k + 1)
        for r in range(reps):
            rel_block(p, rep_peer(r)[0])
        s1_copy(p, device, c).start()

    each(cores - 1, s1_start)
    for r in range(reps):
        rel_block(c, rep_peer(r)[0])

    def s1_wait(k):
        p, device = core_peer(k + 1)
        s1_copy(p, device, p).wait_recv()
        for r in range(reps):
            rel_part[c, r] += recv1[p, r]

    each(cores - 1, s1_wait)

    def s2_start(k):
        p, device = rep_peer(k + 1)
        s2_copy(p, device, x).start()

    each(reps - 1, s2_start)

    src_row = frow[0:1, :] + 256.0 * frow[1:2, :]
    for t in range(slots // chunk):
        at = pl.ds(t * chunk, chunk)
        put_split(go_hl, at, gq_s[at, :] * oper_s[at, :])
    grad = fold(dot(onehot(iota((rows, slots), 0), src_row), go_hl[...]))
    gneg_hi, gneg_lo = split(gneg[...])
    neg_to = onehot(iota((rows, edges), 0), neg[...].astype(F32))
    gneg[...] = grad + (dot(neg_to, gneg_hi) + dot(neg_to, gneg_lo))

    def s2_wait(k):
        p, device = rep_peer(k + 1)
        s2_copy(p, device, p).wait_recv()
        rel_part[c, x] += recv2[p]

    each(reps - 1, s2_wait)

    def s3_start(k):
        p, device = z_peer(k + 1)
        s3_copy(p, device, z).start()

    each(zs - 1, s3_start)

    def gather_in(p):
        to = onehot(iota((rows, cap), 0), ids_in[p][:, :cap])
        hi, lo = split(incoming[p])
        gneg[...] += dot(to, hi) + dot(to, lo)

    gather_in(me)

    def gather_peer(k):
        p = owner_peer(k + 1)
        grad_copy(p, p).wait_recv()
        gather_in(p)

    each(n - 1, gather_peer)

    total = gneg[...]
    ada_col = jnp.transpose(jnp.broadcast_to(ada[...], (8, rows)))[:, 0:1]
    ada_new = ada_col + jnp.sum(total * total, axis=1, keepdims=True) * (1.0 / width)
    rows_out[...] = ent[...] - step_size * total / jnp.sqrt(ada_new)
    ada_out[...] = jnp.transpose(jnp.broadcast_to(ada_new, (rows, 128)))[0:1, :]

    rel_out[...] = rel_part[c, x, pl.ds(pl.multiple_of(z * pad, 8), pad)][:shard]

    def s3_wait(k):
        p, device = z_peer(k + 1)
        s3_copy(p, device, p).wait_recv()
        rel_out[...] += recv3[p][:shard]

    each(zs - 1, s3_wait)

    def drain(k):
        p = owner_peer(k + 1)
        ids_copy(p, me).wait_send()
        row_copy(p, me).wait_send()
        grad_copy(p, me).wait_send()

    each(n - 1, drain)

    def drain1(k):
        p, device = core_peer(k + 1)
        s1_copy(p, device, c).wait_send()

    def drain2(k):
        p, device = rep_peer(k + 1)
        s2_copy(p, device, x).wait_send()

    def drain3(k):
        p, device = z_peer(k + 1)
        s3_copy(p, device, z).wait_send()

    each(cores - 1, drain1)
    each(reps - 1, drain2)
    each(zs - 1, drain3)


def edges_neg(neg):
    return float(neg.shape[1])


def body(
    entity_rows,
    adagrad_sum,
    src_local,
    dst_part,
    dst_local,
    rel_ids,
    neg_local,
    edge_count,
    relations,
):
    n = lax.axis_size("owner")
    reps = lax.axis_size("rep")
    subs = lax.axis_size("sub")
    edges = src_local.shape[0]
    rows, width = entity_rows.shape
    rels = relations.shape[0]
    cap = edges // n * 3 // 2
    shard = rels // (n * reps * subs)
    pad = -(-shard // 8) * 8
    cores = subs if subs > 1 else (2 if n % 2 == 0 else 1)
    zs = n if subs > 1 else n // cores
    dims = (n, reps, subs, cores, zs, cap, shard, pad)
    slots = n * cap
    chunk = 256 if slots % 256 == 0 else slots
    vmem = pl.BlockSpec(memory_space=pltpu.VMEM)
    hbm = pl.BlockSpec(memory_space=pltpu.HBM)
    ids_row = pltpu.VMEM((1, edges), jnp.int32)
    dma = pltpu.SemaphoreType.DMA

    def row(a):
        return a.reshape(1, -1)

    rows_new, ada_new, rel_grad = pl.pallas_call(
        functools.partial(kernel, dims),
        out_shape=(
            jax.ShapeDtypeStruct((rows, width), F32),
            jax.ShapeDtypeStruct((1, rows), F32),
            jax.ShapeDtypeStruct((shard, width), F32),
        ),
        in_specs=[hbm] * 7 + [vmem, hbm],
        out_specs=(vmem, vmem, vmem),
        scratch_shapes=[
            pltpu.VMEM((n, 1, 128), F32),
            pltpu.VMEM((n, 1, 128), F32),
            pltpu.VMEM((rows, 2 * width), BF16),
            pltpu.VMEM((rels, 2 * width), BF16),
            pltpu.VMEM((edges, 2 * width), BF16),
            pltpu.VMEM((n, cap, width), F32),
            pltpu.VMEM((n, cap, width), F32),
            pltpu.VMEM((n, cap, width), F32),
            pltpu.VMEM((n, cap, width), F32),
            pltpu.VMEM((slots, width), F32),
            pltpu.VMEM((slots, width), F32),
            pltpu.VMEM((slots, width), F32),
            pltpu.VMEM((slots, width), F32),
            pltpu.VMEM((chunk, 2 * width), BF16),
            pltpu.VMEM((slots, 2 * width), BF16),
            pltpu.VMEM((slots, 1), F32),
            pltpu.VMEM((16, slots), F32),
            pltpu.VMEM((rows, width), F32),
            pltpu.VMEM((cores, reps, zs * pad, width), F32),
            pltpu.VMEM((cores, reps, zs * pad, width), F32),
            pltpu.VMEM((reps, zs * pad, width), F32),
            pltpu.VMEM((zs, pad, width), F32),
            dma((n,)),
            dma((n,)),
            dma((n,)),
            dma((n,)),
            dma((n,)),
            dma((n,)),
            dma((cores,)),
            dma((cores,)),
            dma((reps,)),
            dma((reps,)),
            dma((zs,)),
            dma((zs,)),
            pltpu.VMEM((rows, width), F32),
            pltpu.VMEM((1, rows), F32),
            ids_row,
            ids_row,
            ids_row,
            ids_row,
            ids_row,
            pltpu.VMEM((rels, width), F32),
            dma((8,)),
        ],
        compiler_params=pltpu.CompilerParams(
            collective_id=0, has_side_effects=True, vmem_limit_bytes=62 * 1024 * 1024
        ),
        cost_estimate=pl.CostEstimate(
            flops=10_000_000_000, bytes_accessed=3_000_000, transcendentals=400_000
        ),
    )(
        entity_rows,
        row(adagrad_sum),
        row(src_local),
        row(dst_part),
        row(dst_local),
        row(rel_ids),
        row(neg_local),
        row(edge_count),
        relations,
    )
    return rows_new, ada_new.reshape(-1), rel_grad


def solution(mesh):
    split_rows = P(("parts", "owner", "rep", "sub"))
    split_wide = P(("parts", "owner", "rep", "sub"), None)
    in_specs = (
        split_wide,
        split_rows,
        split_rows,
        split_wide,
        split_rows,
        split_rows,
        split_rows,
        split_rows,
        P(),
    )
    out_specs = (split_wide, split_rows, split_wide)
    return jax.shard_map(body, mesh=mesh, in_specs=in_specs, out_specs=out_specs, check_vma=False)
```

```python
import functools

import jax
import jax.numpy as jnp
from jax import lax
from jax.experimental import pallas as pl
from jax.experimental.pallas import tpu as pltpu
from jax.sharding import PartitionSpec as P

step_size = 0.1
F32 = jnp.float32
BF16 = jnp.bfloat16
MESH = pl.DeviceIdType.MESH


def iota(shape, dim):
    return lax.broadcasted_iota(jnp.int32, shape, dim).astype(F32)


def dot(a, b):
    return lax.dot_general(a, b, (((1,), (0,)), ((), ())), preferred_element_type=F32)


def dot_nt(a, b):
    return lax.dot_general(a, b, (((1,), (1,)), ((), ())), preferred_element_type=F32)


def split(x):
    hi = x.astype(BF16)
    return hi, (x - hi.astype(F32)).astype(BF16)


def put_split(ref, rows, x):
    width = x.shape[1]
    hi, lo = split(x)
    ref[rows, 0:width] = hi
    ref[rows, width:] = lo


def fold(x):
    width = x.shape[1] // 2
    return x[:, :width] + x[:, width:]


def onehot(a, b):
    return jnp.where(a == b, 1.0, 0.0).astype(BF16)


def each(count, step):
    if count <= 8:
        for k in range(count):
            step(k)
    else:

        @pl.loop(0, count)
        def _(k):
            step(k)


def kernel(
    dims,
    ent_in,
    ada_in,
    src_in,
    dpart_in,
    dloc_in,
    rel_in,
    neg_in,
    cnt,
    relations_in,
    rows_out,
    ada_out,
    rel_out,
    ids_out,
    ids_in,
    ent_hl,
    rel_hl,
    neg_hl,
    served,
    fetched,
    outgoing,
    incoming,
    q_s,
    source_s,
    oper_s,
    gq_s,
    q_hl,
    go_hl,
    act_s,
    frow,
    gneg,
    rel_part,
    recv1,
    recv2,
    recv3,
    ids_send,
    ids_recv,
    row_send,
    row_recv,
    grad_send,
    grad_recv,
    s1_send,
    s1_recv,
    s2_send,
    s2_recv,
    s3_send,
    s3_recv,
    ent,
    ada,
    src,
    dpart,
    dloc,
    rel,
    neg,
    relations,
    load_sem,
):
    n, reps, subs, cores, zs, cap, shard, pad = dims
    pairs = (
        (dpart_in, dpart),
        (dloc_in, dloc),
        (ent_in, ent),
        (src_in, src),
        (rel_in, rel),
        (neg_in, neg),
        (relations_in, relations),
        (ada_in, ada),
    )
    loads = [
        pltpu.make_async_copy(a, b, load_sem.at[i]) for i, (a, b) in enumerate(pairs)
    ]
    for load in loads:
        load.start()
    me = lax.axis_index("owner")
    x = lax.axis_index("rep")
    edges = src.shape[1]
    rows, width = ent.shape
    slots = n * cap
    rels = relations.shape[0]
    chunk = 256 if slots % 256 == 0 else slots
    if subs > 1:
        c, z = lax.axis_index("sub"), me
    else:
        c, z = lax.rem(me, cores), lax.div(me, cores)

    def owner_peer(k):
        return lax.rem(me + n // 2 + (k // 2 if k % 2 == 0 else -(k // 2)) + n, n) if n <= 8 else lax.rem(me + k, n)

    def core_peer(k):
        p = lax.rem(c + k, cores)
        return p, ({"sub": p} if subs > 1 else {"owner": z * cores + p})

    def rep_peer(k):
        p = lax.rem(x + k, reps)
        return p, {"rep": p}

    def z_peer(k):
        p = lax.rem(z + k, zs)
        return p, ({"owner": p} if subs > 1 else {"owner": p * cores + c})

    barrier = pltpu.get_barrier_semaphore()

    def greet(device):
        pl.semaphore_signal(barrier, inc=1, device_id=device, device_id_type=MESH)

    each(n - 1, lambda k: greet({"owner": owner_peer(k + 1)}))
    each(reps - 1, lambda k: greet(rep_peer(k + 1)[1]))
    greeted = n - 1 + reps - 1
    if subs > 1:
        each(subs - 1, lambda k: greet(core_peer(k + 1)[1]))
        greeted += subs - 1

    def copy(source, target, send, recv, device):
        return pltpu.make_async_remote_copy(
            src_ref=source,
            dst_ref=target,
            send_sem=send,
            recv_sem=recv,
            device_id=device,
            device_id_type=MESH,
        )

    def ids_copy(p, s):
        return copy(ids_out.at[p], ids_in.at[s], ids_send.at[p], ids_recv.at[s], {"owner": p})

    def row_copy(p, s):
        return copy(served.at[p], fetched.at[s], row_send.at[p], row_recv.at[s], {"owner": p})

    def grad_copy(p, s):
        return copy(outgoing.at[p], incoming.at[s], grad_send.at[p], grad_recv.at[s], {"owner": p})

    loads[0].wait()
    loads[1].wait()
    dpart_row = dpart[...].astype(F32)
    pt = iota((n, edges), 0) == dpart_row
    before = dot(
        jnp.where(pt, 1.0, 0.0).astype(BF16),
        jnp.where(iota((edges, edges), 0) < iota((edges, edges), 1), 1.0, 0.0).astype(BF16),
    )
    rank = jnp.sum(jnp.where(pt, before, 0.0), axis=0, keepdims=True)
    slot_row = dpart_row * cap + rank

    def low_high(ref):
        v = ref[...]
        return (v & 255).astype(F32), (v >> 8).astype(F32)

    rt = onehot(iota((128, edges), 0), rank)
    low, high = low_high(dloc)
    wanted = dot_nt(jnp.where(pt, low, 0.0).astype(BF16), rt) + 256.0 * dot_nt(
        jnp.where(pt, high, 0.0).astype(BF16), rt
    )
    for p in range(n):
        ids_out[p] = wanted[p : p + 1, :]
    pl.semaphore_wait(barrier, greeted)
    each(n - 1, lambda k: ids_copy(owner_peer(k + 1), me).start())
    ids_in[me] = ids_out[me]

    loads[2].wait()
    put_split(ent_hl, pl.ds(0, rows), ent[...])

    def id_column(s):
        return jnp.transpose(jnp.broadcast_to(ids_in[s], (8, 128)))[:cap, 0:1]

    def serve(s):
        return fold(dot(onehot(id_column(s), iota((cap, rows), 1)), ent_hl[...]))

    def serve_peer(k):
        p = owner_peer(k + 1)
        ids_copy(p, p).wait_recv()
        served[p] = serve(p)
        row_copy(p, me).start()

    each(n - 1, serve_peer)
    fetched[me] = serve(me)

    for load in loads[3:]:
        load.wait()
    src_low, src_high = low_high(src)
    rel_low, rel_high = low_high(rel)
    active = jnp.where(
        lax.broadcasted_iota(jnp.int32, (1, edges), 1) < cnt[...], 1.0, 0.0
    )
    fields = jnp.concatenate(
        [src_low, src_high, rel_low, rel_high, active, jnp.zeros((11, edges), F32)], axis=0
    ).astype(BF16)
    for t in range(rels // 256):
        put_split(rel_hl, pl.ds(t * 256, 256), relations[pl.ds(t * 256, 256), :])
    neg_col = jnp.transpose(jnp.broadcast_to(neg[...].astype(F32), (8, edges)))[:, 0:1]
    neg_hl[...] = dot(onehot(neg_col, iota((edges, rows), 1)), ent_hl[...]).astype(BF16)
    gneg[...] = jnp.zeros_like(gneg)

    @pl.loop(0, slots // chunk)
    def _(t):
        at = pl.ds(pl.multiple_of(t * chunk, chunk), chunk)
        first = (t * chunk).astype(F32)
        st = onehot(iota((chunk, edges), 0) + first, slot_row)
        fcol = dot_nt(st, fields)
        frow[:, at] = dot_nt(fields, st)
        src_col = fcol[:, 0:1] + 256.0 * fcol[:, 1:2]
        rel_col = fcol[:, 2:3] + 256.0 * fcol[:, 3:4]
        act_col = fcol[:, 4:5]
        act_s[at, :] = act_col
        source = fold(dot(onehot(src_col, iota((chunk, rows), 1)), ent_hl[...]))
        operator = fold(dot(onehot(rel_col, iota((chunk, rels), 1)), rel_hl[...]))
        queries = source * operator
        source_s[at, :] = source
        oper_s[at, :] = operator
        q_s[at, :] = queries
        q_hi, q_lo = split(queries)
        q_hl[:, :width] = q_hi
        q_hl[:, width:] = q_lo
        n_hi = neg_hl[:, :width]
        n_lo = neg_hl[:, width:]
        scores = dot_nt(q_hi, n_hi) + (dot_nt(q_hi, n_lo) + dot_nt(q_lo, n_hi))
        gn = jax.nn.sigmoid(scores) * (act_col / edges_neg(neg))
        gn_hi, gn_lo = split(gn)
        gq_s[at, :] = fold(dot(gn_hi, neg_hl[...])) + dot(gn_lo, n_hi)
        gt_hi, gt_lo = split(jnp.transpose(gn))
        gneg[...] += fold(dot(gt_hi, q_hl[...])) + dot(gt_lo, q_hi)

    def block_rows(p):
        return pl.ds(pl.multiple_of(p * cap, 8), cap)

    def score(p, out):
        at = block_rows(p)
        target = fetched[p]
        queries = q_s[at, :]
        positive = jnp.sum(queries * target, axis=1, keepdims=True)
        grad_pos = -jax.nn.sigmoid(-positive) * act_s[at, :]
        out[...] = grad_pos * queries
        gq_s[at, :] += grad_pos * target

    score(me, incoming.at[me])

    def score_peer(k):
        p = owner_peer(n - 1 - k)
        row_copy(p, p).wait_recv()
        score(p, outgoing.at[p])
        grad_copy(p, me).start()

    each(n - 1, score_peer)

    for t in range(slots // chunk):
        at = pl.ds(t * chunk, chunk)
        put_split(go_hl, at, gq_s[at, :] * source_s[at, :])
    rel_row = frow[2:3, :] + 256.0 * frow[3:4, :]
    block = zs * pad

    def rel_block(cc, xx):
        local = iota((block, 1), 0)
        zz = jnp.floor((local + 0.5) * (1.0 / pad))
        within = local - zz * pad
        cf, xf = cc.astype(F32), xx.astype(F32)
        if subs > 1:
            dev = (zz * reps + xf) * subs + cf
        else:
            dev = (zz * cores + cf) * reps + xf
        ident = jnp.where(within < shard, dev * shard + within, -1.0)
        rel_part[cc, xx] = fold(dot(onehot(ident, rel_row), go_hl[...]))

    def s1_copy(p, device, s):
        return copy(rel_part.at[p], recv1.at[s], s1_send.at[p], s1_recv.at[s], device)

    def s2_copy(p, device, s):
        return copy(rel_part.at[c, p], recv2.at[s], s2_send.at[p], s2_recv.at[s], device)

    def s3_copy(p, device, s):
        return copy(
            rel_part.at[c, x, pl.ds(pl.multiple_of(p * pad, 8), pad)],
            recv3.at[s],
            s3_send.at[p],
            s3_recv.at[s],
            device,
        )

    def s1_start(k):
        p, device = core_peer(k + 1)
        for r in range(reps):
            rel_block(p, rep_peer(r)[0])
        s1_copy(p, device, c).start()

    each(cores - 1, s1_start)
    for r in range(reps):
        rel_block(c, rep_peer(r)[0])

    def s1_wait(k):
        p, device = core_peer(k + 1)
        s1_copy(p, device, p).wait_recv()
        for r in range(reps):
            rel_part[c, r] += recv1[p, r]

    each(cores - 1, s1_wait)

    def s2_start(k):
        p, device = rep_peer(k + 1)
        s2_copy(p, device, x).start()

    each(reps - 1, s2_start)

    src_row = frow[0:1, :] + 256.0 * frow[1:2, :]
    for t in range(slots // chunk):
        at = pl.ds(t * chunk, chunk)
        put_split(go_hl, at, gq_s[at, :] * oper_s[at, :])
    grad = fold(dot(onehot(iota((rows, slots), 0), src_row), go_hl[...]))
    gneg_hi, gneg_lo = split(gneg[...])
    neg_to = onehot(iota((rows, edges), 0), neg[...].astype(F32))
    gneg[...] = grad + (dot(neg_to, gneg_hi) + dot(neg_to, gneg_lo))

    def s2_wait(k):
        p, device = rep_peer(k + 1)
        s2_copy(p, device, p).wait_recv()
        rel_part[c, x] += recv2[p]

    each(reps - 1, s2_wait)

    def s3_start(k):
        p, device = z_peer(k + 1)
        s3_copy(p, device, z).start()

    each(zs - 1, s3_start)

    def gather_in(p):
        to = onehot(iota((rows, cap), 0), ids_in[p][:, :cap])
        hi, lo = split(incoming[p])
        gneg[...] += dot(to, hi) + dot(to, lo)

    gather_in(me)

    def gather_peer(k):
        p = owner_peer(k + 1)
        grad_copy(p, p).wait_recv()
        gather_in(p)

    each(n - 1, gather_peer)

    total = gneg[...]
    ada_col = jnp.transpose(jnp.broadcast_to(ada[...], (8, rows)))[:, 0:1]
    ada_new = ada_col + jnp.sum(total * total, axis=1, keepdims=True) * (1.0 / width)
    rows_out[...] = ent[...] - step_size * total / jnp.sqrt(ada_new)
    ada_out[...] = jnp.transpose(jnp.broadcast_to(ada_new, (rows, 128)))[0:1, :]

    rel_out[...] = rel_part[c, x, pl.ds(pl.multiple_of(z * pad, 8), pad)][:shard]

    def s3_wait(k):
        p, device = z_peer(k + 1)
        s3_copy(p, device, p).wait_recv()
        rel_out[...] += recv3[p][:shard]

    each(zs - 1, s3_wait)

    def drain(k):
        p = owner_peer(k + 1)
        ids_copy(p, me).wait_send()
        row_copy(p, me).wait_send()
        grad_copy(p, me).wait_send()

    each(n - 1, drain)

    def drain1(k):
        p, device = core_peer(k + 1)
        s1_copy(p, device, c).wait_send()

    def drain2(k):
        p, device = rep_peer(k + 1)
        s2_copy(p, device, x).wait_send()

    def drain3(k):
        p, device = z_peer(k + 1)
        s3_copy(p, device, z).wait_send()

    each(cores - 1, drain1)
    each(reps - 1, drain2)
    each(zs - 1, drain3)


def edges_neg(neg):
    return float(neg.shape[1])


def body(
    entity_rows,
    adagrad_sum,
    src_local,
    dst_part,
    dst_local,
    rel_ids,
    neg_local,
    edge_count,
    relations,
):
    n = lax.axis_size("owner")
    reps = lax.axis_size("rep")
    subs = lax.axis_size("sub")
    edges = src_local.shape[0]
    rows, width = entity_rows.shape
    rels = relations.shape[0]
    cap = edges // n * 3 // 2
    shard = rels // (n * reps * subs)
    pad = -(-shard // 8) * 8
    cores = subs if subs > 1 else (2 if n % 2 == 0 else 1)
    zs = n if subs > 1 else n // cores
    dims = (n, reps, subs, cores, zs, cap, shard, pad)
    slots = n * cap
    chunk = 256 if slots % 256 == 0 else slots
    vmem = pl.BlockSpec(memory_space=pltpu.VMEM)
    hbm = pl.BlockSpec(memory_space=pltpu.HBM)
    ids_row = pltpu.VMEM((1, edges), jnp.int32)
    dma = pltpu.SemaphoreType.DMA

    def row(a):
        return a.reshape(1, -1)

    rows_new, ada_new, rel_grad = pl.pallas_call(
        functools.partial(kernel, dims),
        out_shape=(
            jax.ShapeDtypeStruct((rows, width), F32),
            jax.ShapeDtypeStruct((1, rows), F32),
            jax.ShapeDtypeStruct((shard, width), F32),
        ),
        in_specs=[hbm] * 7 + [vmem, hbm],
        out_specs=(vmem, vmem, vmem),
        scratch_shapes=[
            pltpu.VMEM((n, 1, 128), F32),
            pltpu.VMEM((n, 1, 128), F32),
            pltpu.VMEM((rows, 2 * width), BF16),
            pltpu.VMEM((rels, 2 * width), BF16),
            pltpu.VMEM((edges, 2 * width), BF16),
            pltpu.VMEM((n, cap, width), F32),
            pltpu.VMEM((n, cap, width), F32),
            pltpu.VMEM((n, cap, width), F32),
            pltpu.VMEM((n, cap, width), F32),
            pltpu.VMEM((slots, width), F32),
            pltpu.VMEM((slots, width), F32),
            pltpu.VMEM((slots, width), F32),
            pltpu.VMEM((slots, width), F32),
            pltpu.VMEM((chunk, 2 * width), BF16),
            pltpu.VMEM((slots, 2 * width), BF16),
            pltpu.VMEM((slots, 1), F32),
            pltpu.VMEM((16, slots), F32),
            pltpu.VMEM((rows, width), F32),
            pltpu.VMEM((cores, reps, zs * pad, width), F32),
            pltpu.VMEM((cores, reps, zs * pad, width), F32),
            pltpu.VMEM((reps, zs * pad, width), F32),
            pltpu.VMEM((zs, pad, width), F32),
            dma((n,)),
            dma((n,)),
            dma((n,)),
            dma((n,)),
            dma((n,)),
            dma((n,)),
            dma((cores,)),
            dma((cores,)),
            dma((reps,)),
            dma((reps,)),
            dma((zs,)),
            dma((zs,)),
            pltpu.VMEM((rows, width), F32),
            pltpu.VMEM((1, rows), F32),
            ids_row,
            ids_row,
            ids_row,
            ids_row,
            ids_row,
            pltpu.VMEM((rels, width), F32),
            dma((8,)),
        ],
        compiler_params=pltpu.CompilerParams(
            collective_id=0, has_side_effects=True, vmem_limit_bytes=62 * 1024 * 1024
        ),
        cost_estimate=pl.CostEstimate(
            flops=10_000_000_000, bytes_accessed=3_000_000, transcendentals=400_000
        ),
    )(
        entity_rows,
        row(adagrad_sum),
        row(src_local),
        row(dst_part),
        row(dst_local),
        row(rel_ids),
        row(neg_local),
        row(edge_count),
        relations,
    )
    return rows_new, ada_new.reshape(-1), rel_grad


def solution(mesh):
    split_rows = P(("parts", "owner", "rep", "sub"))
    split_wide = P(("parts", "owner", "rep", "sub"), None)
    in_specs = (
        split_wide,
        split_rows,
        split_rows,
        split_wide,
        split_rows,
        split_rows,
        split_rows,
        split_rows,
        P(),
    )
    out_specs = (split_wide, split_rows, split_wide)
    return jax.shard_map(body, mesh=mesh, in_specs=in_specs, out_specs=out_specs, check_vma=False)
```
